256 devices in a mesh: wide: 32 (over z, y), tp: 8 (over x, core).
Axes of the slice: x: 4, y: 4, z: 8, core: 2. Of those that a mesh axis runs over, the one named last changes fastest.
Arguments:
- queries: bfloat16 [16384, 8192], P('wide', 'tp'), may hold values from -8 to 8
- resp_kv: bfloat16 [2, 16384, 1024], P(None, 'wide', 'tp'), may hold values from -8 to 8
- prompt_kv: bfloat16 [2, 65536, 1024], P(None, 'wide', 'tp'), may hold values from -6 to 6
- out_weight: bfloat16 [8192, 4096], P('tp'), may hold values from -0.0625 to 0.0625
- lengths: int32 [128, 4], P('wide'), may hold values from 1 to 64, 128 in all within a row
- group_prompt: int32 [32, 4], P('wide'), may hold values from 0 to 31, as said below
Outputs:
- projected: bfloat16 [16384, 4096], P(('wide', 'tp'))
The draws below stay inside these ranges and needn't reach their ends.
Inputs may be any that keep to these rules, and one draw needn't show every extreme that they name: `group_prompt`: the 4 blocks of index w belong to the prompts w, w - 1, ..., w - 4 + 1 modulo 32, one each, in an order drawn for each w.
All inputs are finite; a program needn't handle non-finite values.
Results may differ from the reference program's by a relative error of at most 0.018.
Values may be sent and summed in bfloat16 or wider, within the bound.
A program may use at most 64 MiB of HBM per device.

```python
import math
import jax
import jax.numpy as jnp
import numpy as np
from jax import lax

HEADS = 64
KV_HEADS = 8
HEAD_DIM = 128
D_OUT = 4096
PROMPT_LEN = 2048
RTOK_DEV = 512
G = 16
REACH = 4
PROMPTS = 32
RTOK = 16384
RUN = 128
MOST_LEN = 64
N_TP = 8


def draw_queries(key, part):
    key = jax.random.fold_in(key, 1)
    result = jax.random.truncated_normal(key, -4.0, 4.0, (RTOK, HEADS * HEAD_DIM), jnp.float32)
    return result.astype(jnp.bfloat16)


def draw_resp_kv(key, part):
    key = jax.random.fold_in(key, 2)
    result = jax.random.truncated_normal(key, -4.0, 4.0, (2, RTOK, KV_HEADS * HEAD_DIM), jnp.float32)
    return result.astype(jnp.bfloat16)


def shuffle_one(subkey):
    return jax.random.permutation(subkey, REACH)


def draw_group_prompt(key, part):
    key = jax.random.fold_in(key, 3)
    owners = jnp.arange(PROMPTS, dtype=jnp.int32)[:, None]
    shuffles = jax.vmap(shuffle_one)(jax.random.split(key, PROMPTS)).astype(jnp.int32)
    return ((owners - shuffles) % PROMPTS).astype(jnp.int32)


def steps_of(own_key, extent, cuts, smallest, top_value):
    level = 1.0
    for axis_at, parts in cuts:
        draws = jax.random.uniform(jax.random.fold_in(jax.random.fold_in(own_key, 6), axis_at), (parts,), jnp.float32, smallest / len(cuts), top_value / len(cuts))
        level = level * jnp.repeat(jnp.exp(draws), extent[axis_at] // parts).reshape((-1,) + (1,) * (len(extent) - 1 - axis_at))
    return level


def length_profile(number_of, total, bound, lean):
    loads = [(1 << 20) // math.isqrt(grade ** lean) + 1 for grade in range(2, number_of + 1)]
    surplus, counts = total - bound - (number_of - 1), [1] * (number_of - 1)
    while surplus > 0:
        free = [i for i in range(number_of - 1) if counts[i] < bound]
        mass, budget = sum([loads[i] for i in free]), surplus
        for i in free:
            extra = min(bound - counts[i], max(1, budget * loads[i] // mass), surplus)
            counts[i] = counts[i] + extra
            surplus = surplus - extra
    return np.array([bound] + counts)


def ragged(stream_key, amount, total, reach, lean):
    if amount == 2:
        one = jax.random.randint(stream_key, (), max(1, total - reach), min(reach, total - 1) + 1)
        return jnp.stack([one, total - one])
    sizes = jnp.asarray(length_profile(amount, total, reach, lean), jnp.int32)
    twos = (amount - 1) // 2
    giver, sink = sizes[1:1 + 2 * twos:2], sizes[2:2 + 2 * twos:2]
    margin = jnp.minimum(giver - 1, reach - sink)
    shifted = jax.random.randint(jax.random.fold_in(stream_key, 1), (twos,), 0, 1 << 20) % (margin + 1)
    sizes = sizes.at[1:1 + 2 * twos:2].set(giver - shifted).at[2:2 + 2 * twos:2].set(sink + shifted)
    return sizes[jax.random.permutation(jax.random.fold_in(stream_key, 2), amount)]


def centred(own_key, dims, scale, bound, pieces=(), kind=jnp.bfloat16):
    array = scale * jax.random.normal(own_key, dims, jnp.float32)
    if pieces:
        array = array * steps_of(own_key, dims, pieces, -0.22, 0.18)
    return jnp.clip(array, -bound, bound).astype(kind)


def setup_inputs(seed: int = 0) -> dict:
    seeds = jax.random.split(jax.random.key(seed), 7)
    return {
        "queries": draw_queries(jax.random.fold_in(seeds[6], 71), 0),
        "resp_kv": draw_resp_kv(jax.random.fold_in(seeds[6], 71), 0),
        "prompt_kv": centred(seeds[2], (2, PROMPTS * PROMPT_LEN, KV_HEADS * HEAD_DIM), 1.0, 6.0, ((1, 32), (2, 8))),
        "out_weight": centred(seeds[3], (HEADS * HEAD_DIM, D_OUT), (HEADS * HEAD_DIM) ** -0.5, 0.0625, ((0, 8),)),
        "lengths": jax.vmap(lambda own: ragged(own, G // REACH, RUN, MOST_LEN, 2))(jax.random.split(seeds[4], (PROMPTS * REACH))).reshape((PROMPTS * REACH, G // REACH)).astype(jnp.int32),
        "group_prompt": draw_group_prompt(jax.random.fold_in(seeds[6], 71), 0),
    }


def attend_block(query_rows, prompt_pair, self_pair, run_lengths):
    run_len = query_rows.shape[0]
    kv_width = prompt_pair.shape[2]
    kv_heads = kv_width // HEAD_DIM
    group_size = query_rows.shape[1] // kv_width
    query_heads = query_rows.astype(jnp.float32).reshape(run_len, kv_heads, group_size, HEAD_DIM)
    prompt_keys = prompt_pair[0].astype(jnp.float32).reshape(-1, kv_heads, HEAD_DIM)
    prompt_vals = prompt_pair[1].astype(jnp.float32).reshape(-1, kv_heads, HEAD_DIM)
    self_keys = self_pair[0].astype(jnp.float32).reshape(-1, kv_heads, HEAD_DIM)
    self_vals = self_pair[1].astype(jnp.float32).reshape(-1, kv_heads, HEAD_DIM)
    score_scale = 1.0 / math.sqrt(HEAD_DIM)
    prompt_score = jnp.einsum('tkgd,skd->kgts', query_heads, prompt_keys) * score_scale
    self_score = jnp.einsum('tkgd,skd->kgts', query_heads, self_keys) * score_scale
    boundary = jnp.cumsum(run_lengths).astype(jnp.int32)
    position = jnp.arange(run_len, dtype=jnp.int32)
    segment = lax.optimization_barrier(jnp.sum((position[:, None] >= boundary[None, :]).astype(jnp.int32), axis=1))
    allowed = (segment[:, None] == segment[None, :]) & (position[None, :] <= position[:, None])
    self_score = jnp.where(allowed, self_score, -jnp.inf)
    highest = jnp.maximum(lax.optimization_barrier(jnp.max(prompt_score, axis=-1)), lax.optimization_barrier(jnp.max(self_score, axis=-1)))[..., None]
    prompt_exp = jnp.exp(prompt_score - highest)
    self_exp = jnp.exp(self_score - highest)
    total_weight = lax.optimization_barrier(jnp.sum(prompt_exp, axis=-1, keepdims=True)) + lax.optimization_barrier(jnp.sum(self_exp, axis=-1, keepdims=True))
    prompt_weight = (prompt_exp / total_weight).astype(jnp.bfloat16)
    self_weight = (self_exp / total_weight).astype(jnp.bfloat16)
    mixed = jnp.einsum('kgts,skd->tkgd', prompt_weight.astype(jnp.float32), prompt_vals)
    mixed = mixed + jnp.einsum('kgts,skd->tkgd', self_weight.astype(jnp.float32), self_vals)
    return mixed.reshape(run_len, -1).astype(jnp.bfloat16)

def reference(queries, resp_kv, prompt_kv, out_weight, lengths, group_prompt):

    def one_index(owner):
        query_rows = lax.dynamic_slice_in_dim(queries, owner * RTOK_DEV, RTOK_DEV, 0)
        self_rows = lax.dynamic_slice_in_dim(resp_kv, owner * RTOK_DEV, RTOK_DEV, 1)
        block_lengths = lax.dynamic_slice_in_dim(lengths, owner * REACH, REACH, 0)
        block_prompts = lax.dynamic_index_in_dim(group_prompt, owner, 0, keepdims=False)

        def one_block(block):
            block_rows = lax.dynamic_slice_in_dim(query_rows, block * RUN, RUN, 0)
            self_pair = lax.dynamic_slice_in_dim(self_rows, block * RUN, RUN, 1)
            prompt_pair = lax.dynamic_slice_in_dim(prompt_kv, block_prompts[block] * PROMPT_LEN, PROMPT_LEN, 1)
            return attend_block(block_rows, prompt_pair, self_pair, block_lengths[block])
        attended = lax.map(one_block, jnp.arange(REACH, dtype=jnp.int32)).reshape(RTOK_DEV, -1)
        head_cols = HEADS * HEAD_DIM // N_TP
        summed = jnp.zeros((RTOK_DEV, D_OUT), jnp.float32)
        for member in range(N_TP):
            partial_sum = jnp.dot(attended[:, member * head_cols:(member + 1) * head_cols], out_weight[member * head_cols:(member + 1) * head_cols], preferred_element_type=jnp.float32)
            summed = summed + lax.optimization_barrier(partial_sum.astype(jnp.bfloat16)).astype(jnp.float32)
        return summed.astype(jnp.bfloat16)
    projected = lax.map(one_index, jnp.arange(PROMPTS, dtype=jnp.int32))
    return projected.reshape(PROMPTS * RTOK_DEV, D_OUT)
```

```python
import functools
import math

import jax
import jax.numpy as jnp
from jax import lax
from jax.experimental import pallas as pl
from jax.experimental.pallas import tpu as pltpu
from jax.sharding import PartitionSpec as P

MESH = pl.DeviceIdType.MESH
HEAD = 128
RUN = 128
HEADS = 8
PROMPT = 2048
KEYS = PROMPT + RUN
D_OUT = 4096
WIDE = 32
CHIPS = 4
HALF = RUN // 2
QUART = D_OUT // CHIPS
CHUNK_HEADS = 4
ROWS = CHUNK_HEADS * RUN
PACK = HEADS * HEAD + 2 * HEAD
EXP_SCALE = math.log2(math.e) / math.sqrt(HEAD)
F32 = jnp.float32
BF16 = jnp.bfloat16


def kernel(
    q_hbm, resp_hbm, prompt_hbm, w_hbm, len_ref, gp_ref,
    out_ref,
    q_buf, resp_buf, keys, vals, w_buf,
    pack_tx, pack_rx, bound_tx, bound_rx, self_vals,
    score0, score1, prob0, prob1, att, part, pair_rx, held, rs_rx, red, home, gather_tx,
    load_sem, pack_send, pack_recv, bound_send, bound_recv,
    pair_send, pair_recv, rs_send, rs_recv, ret_send, ret_recv, gather_send, gather_recv,
):
    wide = lax.axis_index("wide")
    member = lax.axis_index("tp")
    chip = lax.div(member, 2)
    core = lax.rem(member, 2)

    loads = [
        pltpu.make_async_copy(q_hbm, q_buf, load_sem.at[0]),
        pltpu.make_async_copy(resp_hbm, resp_buf, load_sem.at[1]),
        pltpu.make_async_copy(prompt_hbm.at[0], keys, load_sem.at[2]),
        pltpu.make_async_copy(prompt_hbm.at[1], vals.at[:, pl.ds(0, HEAD)], load_sem.at[3]),
        pltpu.make_async_copy(w_hbm, w_buf, load_sem.at[4]),
    ]
    for load in loads:
        load.start()

    def along_wide(steps):
        return {"wide": lax.rem(wide + steps + WIDE, WIDE)}

    def along_chip(steps):
        return {"tp": lax.rem(member + 2 * steps, 2 * CHIPS)}

    sibling = {"tp": member + 1 - 2 * core}

    barrier = pltpu.get_barrier_semaphore()
    partners = [along_wide(s) for s in (-3, -2, -1, 1, 2, 3)] + [along_chip(s) for s in (1, 2, 3)] + [sibling]
    for partner in partners:
        pl.semaphore_signal(barrier, inc=1, device_id=partner, device_id_type=MESH)

    def remote(src, dst, send, recv, device):
        return pltpu.make_async_remote_copy(
            src_ref=src, dst_ref=dst, send_sem=send, recv_sem=recv, device_id=device, device_id_type=MESH
        )

    def slot_at(block):
        return jnp.minimum(lax.rem(wide - gp_ref[0, block] + WIDE, WIDE), 3)

    slot_of = [slot_at(b) for b in range(4)]
    hit = [[1 - jnp.minimum((slot_of[b] - k) * (slot_of[b] - k), 1) for b in range(4)] for k in range(4)]
    block_of = [jnp.minimum(hit[k][1] + 2 * hit[k][2] + 3 * hit[k][3], 3) for k in range(4)]

    vals[:, pl.ds(HEAD, HEAD)] = jnp.ones((PROMPT, HEAD), BF16)
    for s in range(4):
        self_vals[s, :, pl.ds(HEAD, HEAD)] = jnp.ones((RUN, HEAD), BF16)

    loads[0].wait()
    loads[1].wait()
    line = lax.broadcasted_iota(jnp.int32, (8, 128), 0)
    for k in (1, 3, 2, 0):
        target = pack_rx if k == 0 else pack_tx
        bounds = bound_rx if k == 0 else bound_tx
        target[k, :, pl.ds(0, HEADS * HEAD)] = q_buf[block_of[k]]
        target[k, :, pl.ds(HEADS * HEAD, HEAD)] = resp_buf[0, block_of[k]]
        target[k, :, pl.ds((HEADS + 1) * HEAD, HEAD)] = resp_buf[1, block_of[k]]
        first = sum(hit[k][b] * len_ref[b, 0] for b in range(4))
        second = first + sum(hit[k][b] * len_ref[b, 1] for b in range(4))
        third = second + sum(hit[k][b] * len_ref[b, 2] for b in range(4))
        bounds[k] = jnp.where(line == 0, first, jnp.where(line == 1, second, third))

    pl.semaphore_wait(barrier, len(partners))

    packs, bnds = {}, {}
    for k in (1, 2, 3):
        packs[k] = remote(pack_tx.at[k], pack_rx.at[k], pack_send.at[k], pack_recv.at[k], along_wide(-k))
        bnds[k] = remote(bound_tx.at[k], bound_rx.at[k], bound_send.at[k], bound_recv.at[k], along_wide(-k))
    for k in (1, 3):
        bnds[k].start()
        packs[k].start()

    def arrive(s):
        if s:
            bnds[s].wait_recv()
            packs[s].wait_recv()

    def make_scores(s, chunk, score):
        rows = jnp.concatenate(
            [pack_rx[s, :, pl.ds((chunk * CHUNK_HEADS + j) * HEAD, HEAD)] for j in range(CHUNK_HEADS)], axis=0
        )
        dims = (((1,), (1,)), ((), ()))
        score[:, pl.ds(0, PROMPT)] = lax.dot_general(rows, keys[...], dims, preferred_element_type=F32)
        score[:, pl.ds(PROMPT, RUN)] = lax.dot_general(
            rows, pack_rx[s, :, pl.ds(HEADS * HEAD, HEAD)], dims, preferred_element_type=F32
        )

    def make_mask(s):
        at = lax.broadcasted_iota(jnp.int32, (RUN, RUN), 0)
        key_at = lax.broadcasted_iota(jnp.int32, (RUN, RUN), 1)
        begin = jnp.zeros((RUN, RUN), jnp.int32)
        for j in range(3):
            edge = bound_rx[s, pl.ds(j, 1), :]
            begin = jnp.maximum(begin, jnp.where(at >= edge, edge, 0))
        return (key_at >= begin) & (key_at <= at)

    def finish(s, chunk, score, prob):
        mask = make_mask(s)
        for j in range(CHUNK_HEADS):
            here = pl.ds(j * RUN, RUN)
            far = score[here, pl.ds(0, PROMPT)]
            near = jnp.where(mask, score[here, pl.ds(PROMPT, RUN)], -jnp.inf)
            top = jnp.maximum(jnp.max(far, axis=1, keepdims=True), jnp.max(near, axis=1, keepdims=True))
            top = top * EXP_SCALE
            prob[here, pl.ds(0, PROMPT)] = jnp.exp2(far * EXP_SCALE - top).astype(BF16)
            prob[here, pl.ds(PROMPT, RUN)] = jnp.exp2(near * EXP_SCALE - top).astype(BF16)
        mixed = jnp.dot(prob[:, pl.ds(0, PROMPT)], vals[...], preferred_element_type=F32)
        mixed = mixed + jnp.dot(prob[:, pl.ds(PROMPT, RUN)], self_vals[s], preferred_element_type=F32)
        result = (mixed[:, :HEAD] / mixed[:, HEAD:]).astype(BF16)
        for j in range(CHUNK_HEADS):
            att[s, :, pl.ds((chunk * CHUNK_HEADS + j) * HEAD, HEAD)] = result[j * RUN:(j + 1) * RUN]

    def attend(s):
        self_vals[s, :, pl.ds(0, HEAD)] = pack_rx[s, :, pl.ds((HEADS + 1) * HEAD, HEAD)]
        make_scores(s, 0, score0)
        make_scores(s, 1, score1)
        finish(s, 0, score0, prob0)
        finish(s, 1, score1, prob1)

    pairs = {}

    def project(s):
        def columns(i, carry):
            cols = pl.ds(pl.multiple_of(i * QUART, QUART), QUART)
            part[s, :, cols] = jnp.dot(att[s], w_buf[:, cols], preferred_element_type=F32).astype(BF16)
            return carry

        lax.fori_loop(0, D_OUT // QUART, columns, 0)
        theirs = pl.ds(pl.multiple_of((1 - core) * HALF, HALF), HALF)
        pairs[s] = remote(part.at[s, theirs], pair_rx.at[s], pair_send.at[s], pair_recv.at[s], sibling)
        pairs[s].start()

    rs = {}

    def combine(s):
        pairs[s].wait_recv()
        mine = pl.ds(pl.multiple_of(core * HALF, HALF), HALF)
        held[s] = (part[s, mine, :].astype(F32) + pair_rx[s].astype(F32)).astype(BF16)
        for j in (1, 3, 2):
            there = lax.rem(chip + j, CHIPS)
            cols = pl.ds(pl.multiple_of(there * QUART, QUART), QUART)
            rs[s, j] = remote(
                held.at[s, :, cols], rs_rx.at[s, j], rs_send.at[s, j], rs_recv.at[s, j], along_chip(j)
            )
            rs[s, j].start()

    returns = {}

    def reduce(s):
        for j in (1, 3, 2):
            rs[s, j].wait_recv()
        cols = pl.ds(pl.multiple_of(chip * QUART, QUART), QUART)
        total = held[s, :, cols].astype(F32)
        for j in (1, 2, 3):
            total = total + rs_rx[s, j].astype(F32)
        if s == 0:
            home[0] = total.astype(BF16)
        else:
            red[s] = total.astype(BF16)
            returns[s] = remote(red.at[s], home.at[s], ret_send.at[s], ret_recv.at[s], along_wide(s))
            returns[s].start()

    loads[2].wait()
    loads[3].wait()
    attend(0)
    for k in (1, 3):
        bnds[k].wait_send()
        packs[k].wait_send()
    bnds[2].start()
    packs[2].start()
    loads[4].wait()
    project(0)
    arrive(1)
    attend(1)
    combine(0)
    project(1)
    arrive(3)
    attend(3)
    combine(1)
    project(3)
    reduce(0)
    reduce(1)
    arrive(2)
    attend(2)
    combine(3)
    project(2)
    reduce(3)
    combine(2)
    reduce(2)

    for k in (1, 2, 3):
        returns[k].wait_recv()

    mine = pl.ds(pl.multiple_of(chip * QUART, QUART), QUART)
    gathers = []
    for j in (1, 3, 2):
        there = lax.rem(chip + j, CHIPS)
        gather_tx[j] = home[slot_at(there)]
        copy = remote(gather_tx.at[j], out_ref.at[:, mine], gather_send.at[j], gather_recv.at[j], along_chip(j))
        copy.start()
        gathers.append(copy)
    out_ref[:, mine] = home[slot_at(chip)]

    bnds[2].wait_send()
    packs[2].wait_send()
    for s in range(4):
        pairs[s].wait_send()
        for j in (1, 2, 3):
            rs[s, j].wait_send()
        if s:
            returns[s].wait_send()
    for copy in gathers:
        copy.wait_send()
        copy.wait_recv()


def body(queries, resp_kv, prompt_kv, out_weight, lengths, group_prompt):
    queries = queries.reshape(4, RUN, HEADS * HEAD)
    resp_kv = resp_kv.reshape(2, 4, RUN, HEAD)
    hbm = pl.BlockSpec(memory_space=pl.ANY)
    smem = pl.BlockSpec(memory_space=pltpu.SMEM)
    dma = pltpu.SemaphoreType.DMA
    return pl.pallas_call(
        kernel,
        out_shape=jax.ShapeDtypeStruct((HALF, D_OUT), BF16),
        in_specs=[hbm, hbm, hbm, hbm, smem, smem],
        out_specs=pl.BlockSpec(memory_space=pltpu.VMEM),
        scratch_shapes=[
            pltpu.VMEM((4, RUN, HEADS * HEAD), BF16),
            pltpu.VMEM((2, 4, RUN, HEAD), BF16),
            pltpu.VMEM((PROMPT, HEAD), BF16),
            pltpu.VMEM((PROMPT, 2 * HEAD), BF16),
            pltpu.VMEM((HEADS * HEAD, D_OUT), BF16),
            pltpu.VMEM((4, RUN, PACK), BF16),
            pltpu.VMEM((4, RUN, PACK), BF16),
            pltpu.VMEM((4, 8, 128), jnp.int32),
            pltpu.VMEM((4, 8, 128), jnp.int32),
            pltpu.VMEM((4, RUN, 2 * HEAD), BF16),
            pltpu.VMEM((ROWS, KEYS), F32),
            pltpu.VMEM((ROWS, KEYS), F32),
            pltpu.VMEM((ROWS, KEYS), BF16),
            pltpu.VMEM((ROWS, KEYS), BF16),
            pltpu.VMEM((4, RUN, HEADS * HEAD), BF16),
            pltpu.VMEM((4, RUN, D_OUT), BF16),
            pltpu.VMEM((4, HALF, D_OUT), BF16),
            pltpu.VMEM((4, HALF, D_OUT), BF16),
            pltpu.VMEM((4, 4, HALF, QUART), BF16),
            pltpu.VMEM((4, HALF, QUART), BF16),
            pltpu.VMEM((4, HALF, QUART), BF16),
            pltpu.VMEM((4, HALF, QUART), BF16),
            dma((5,)),
            dma((4,)), dma((4,)), dma((4,)), dma((4,)),
            dma((4,)), dma((4,)), dma((4, 4)), dma((4, 4)), dma((4,)), dma((4,)), dma((4,)), dma((4,)),
        ],
        compiler_params=pltpu.CompilerParams(
            collective_id=1, has_side_effects=True, vmem_limit_bytes=60 * 1024 * 1024
        ),
        cost_estimate=pl.CostEstimate(flops=9 * 10**9, bytes_accessed=12 * 2**20, transcendentals=9 * 10**6),
    )(queries, resp_kv, prompt_kv, out_weight, lengths, group_prompt)


def solution(mesh):
    placed = (
        P("wide", "tp"),
        P(None, "wide", "tp"),
        P(None, "wide", "tp"),
        P("tp", None),
        P("wide", None),
        P("wide", None),
    )
    return jax.shard_map(
        body, mesh=mesh, in_specs=placed, out_specs=P(("wide", "tp"), None), check_vma=False
    )
```

```python
import functools
import math

import jax
import jax.numpy as jnp
from jax import lax
from jax.experimental import pallas as pl
from jax.experimental.pallas import tpu as pltpu
from jax.sharding import PartitionSpec as P

MESH = pl.DeviceIdType.MESH
HEAD = 128
RUN = 128
HEADS = 8
PROMPT = 2048
KEYS = PROMPT + RUN
D_OUT = 4096
WIDE = 32
CHIPS = 4
HALF = RUN // 2
QUART = D_OUT // CHIPS
CHUNK_HEADS = 4
ROWS = CHUNK_HEADS * RUN
PACK = HEADS * HEAD + 2 * HEAD
EXP_SCALE = math.log2(math.e) / math.sqrt(HEAD)
F32 = jnp.float32
BF16 = jnp.bfloat16


def kernel(
    q_hbm, resp_hbm, prompt_hbm, w_hbm, len_ref, gp_ref,
    out_ref,
    q_buf, resp_buf, keys, vals, w_buf,
    pack_tx, pack_rx, bound_tx, bound_rx, self_vals,
    score0, score1, prob0, prob1, att, part, pair_rx, held, relay_rx, relay_tx, sum_rx, red, home, gather_tx,
    load_sem, pack_send, pack_recv, bound_send, bound_recv,
    pair_send, pair_recv, rs_send, rs_recv, ret_send, ret_recv, gather_send, gather_recv,
):
    wide = lax.axis_index("wide")
    member = lax.axis_index("tp")
    chip = lax.div(member, 2)
    core = lax.rem(member, 2)

    loads = [
        pltpu.make_async_copy(q_hbm, q_buf, load_sem.at[0]),
        pltpu.make_async_copy(resp_hbm, resp_buf, load_sem.at[1]),
        pltpu.make_async_copy(prompt_hbm.at[0], keys, load_sem.at[2]),
        pltpu.make_async_copy(prompt_hbm.at[1], vals.at[:, pl.ds(0, HEAD)], load_sem.at[3]),
        pltpu.make_async_copy(w_hbm, w_buf, load_sem.at[4]),
    ]
    for load in loads[:4]:
        load.start()

    def along_wide(steps):
        return {"wide": lax.rem(wide + steps + WIDE, WIDE)}

    def along_chip(steps):
        return {"tp": lax.rem(member + 2 * steps, 2 * CHIPS)}

    sibling = {"tp": member + 1 - 2 * core}

    barrier = pltpu.get_barrier_semaphore()
    partners = [along_wide(s) for s in (-3, -2, -1, 1, 2, 3)] + [along_chip(s) for s in (1, 2, 3)] + [sibling]
    for partner in partners:
        pl.semaphore_signal(barrier, inc=1, device_id=partner, device_id_type=MESH)

    def remote(src, dst, send, recv, device):
        return pltpu.make_async_remote_copy(
            src_ref=src, dst_ref=dst, send_sem=send, recv_sem=recv, device_id=device, device_id_type=MESH
        )

    def slot_at(block):
        return jnp.minimum(lax.rem(wide - gp_ref[0, block] + WIDE, WIDE), 3)

    slot_of = [slot_at(b) for b in range(4)]
    hit = [[1 - jnp.minimum((slot_of[b] - k) * (slot_of[b] - k), 1) for b in range(4)] for k in range(4)]
    block_of = [jnp.minimum(hit[k][1] + 2 * hit[k][2] + 3 * hit[k][3], 3) for k in range(4)]

    vals[:, pl.ds(HEAD, HEAD)] = jnp.ones((PROMPT, HEAD), BF16)
    for s in range(4):
        self_vals[s, :, pl.ds(HEAD, HEAD)] = jnp.ones((RUN, HEAD), BF16)

    loads[0].wait()
    loads[1].wait()
    loads[4].start()
    line = lax.broadcasted_iota(jnp.int32, (8, 128), 0)

    def stage(k):
        target = pack_rx if k == 0 else pack_tx
        bounds = bound_rx if k == 0 else bound_tx
        target[k, :, pl.ds(0, HEADS * HEAD)] = q_buf[block_of[k]]
        target[k, :, pl.ds(HEADS * HEAD, HEAD)] = resp_buf[0, block_of[k]]
        target[k, :, pl.ds((HEADS + 1) * HEAD, HEAD)] = resp_buf[1, block_of[k]]
        first = sum(hit[k][b] * len_ref[b, 0] for b in range(4))
        second = first + sum(hit[k][b] * len_ref[b, 1] for b in range(4))
        third = second + sum(hit[k][b] * len_ref[b, 2] for b in range(4))
        bounds[k] = jnp.where(line == 0, first, jnp.where(line == 1, second, third))

    bnds = {
        k: remote(bound_tx.at[k], bound_rx.at[k], bound_send.at[k], bound_recv.at[k], along_wide(-k)) for k in (1, 2, 3)
    }
    packs = {
        k: remote(pack_tx.at[k], pack_rx.at[k], pack_send.at[k], pack_recv.at[k], along_wide(-k)) for k in (1, 2, 3)
    }

    stage(1)
    pl.semaphore_wait(barrier, len(partners))

    packs[1].start()
    stage(3)
    packs[3].start()
    bnds[1].start()
    bnds[3].start()
    stage(0)

    def arrive(s):
        bnds[s].wait_recv()
        packs[s].wait_recv()

    def make_scores(s, chunk, score):
        rows = jnp.concatenate(
            [pack_rx[s, :, pl.ds((chunk * CHUNK_HEADS + j) * HEAD, HEAD)] for j in range(CHUNK_HEADS)], axis=0
        )
        dims = (((1,), (1,)), ((), ()))
        score[:, pl.ds(0, PROMPT)] = lax.dot_general(rows, keys[...], dims, preferred_element_type=F32)
        score[:, pl.ds(PROMPT, RUN)] = lax.dot_general(
            rows, pack_rx[s, :, pl.ds(HEADS * HEAD, HEAD)], dims, preferred_element_type=F32
        )

    def make_mask(s):
        at = lax.broadcasted_iota(jnp.int32, (RUN, RUN), 0)
        key_at = lax.broadcasted_iota(jnp.int32, (RUN, RUN), 1)
        begin = jnp.zeros((RUN, RUN), jnp.int32)
        for j in range(3):
            edge = bound_rx[s, pl.ds(j, 1), :]
            begin = jnp.maximum(begin, jnp.where(at >= edge, edge, 0))
        return (key_at >= begin) & (key_at <= at)

    def finish(s, chunk, score, prob):
        mask = make_mask(s)
        for j in range(CHUNK_HEADS):
            here = pl.ds(j * RUN, RUN)
            far = score[here, pl.ds(0, PROMPT)]
            near = jnp.where(mask, score[here, pl.ds(PROMPT, RUN)], -jnp.inf)
            top = jnp.maximum(jnp.max(far, axis=1, keepdims=True), jnp.max(near, axis=1, keepdims=True))
            top = top * EXP_SCALE
            prob[here, pl.ds(0, PROMPT)] = jnp.exp2(far * EXP_SCALE - top).astype(BF16)
            prob[here, pl.ds(PROMPT, RUN)] = jnp.exp2(near * EXP_SCALE - top).astype(BF16)
        mixed = jnp.dot(prob[:, pl.ds(0, PROMPT)], vals[...], preferred_element_type=F32)
        mixed = mixed + jnp.dot(prob[:, pl.ds(PROMPT, RUN)], self_vals[s], preferred_element_type=F32)
        result = (mixed[:, :HEAD] / mixed[:, HEAD:]).astype(BF16)
        for j in range(CHUNK_HEADS):
            att[s, :, pl.ds((chunk * CHUNK_HEADS + j) * HEAD, HEAD)] = result[j * RUN:(j + 1) * RUN]

    def attend(s):
        self_vals[s, :, pl.ds(0, HEAD)] = pack_rx[s, :, pl.ds((HEADS + 1) * HEAD, HEAD)]
        make_scores(s, 0, score0)
        make_scores(s, 1, score1)
        finish(s, 0, score0, prob0)
        finish(s, 1, score1, prob1)

    ahead, behind = lax.rem(chip + 1, CHIPS), lax.rem(chip + CHIPS - 1, CHIPS)
    across = lax.rem(chip + 2, CHIPS)
    mine = pl.ds(pl.multiple_of(core * HALF, HALF), HALF)
    theirs = pl.ds(pl.multiple_of((1 - core) * HALF, HALF), HALF)

    def quarter(there):
        return pl.ds(pl.multiple_of(there * QUART, QUART), QUART)

    def eighth(there, half):
        return pl.ds(pl.multiple_of(there * QUART + half * (QUART // 2), QUART // 2), QUART // 2)

    pairs, rs = {}, {}

    def project(s, i, there):
        cols = quarter(there)
        part[s, :, cols] = jnp.dot(att[s], w_buf[:, cols], preferred_element_type=F32).astype(BF16)
        pairs[s, i] = remote(
            part.at[s, theirs, cols], pair_rx.at[s, :, cols], pair_send.at[s, i], pair_recv.at[s, i], sibling
        )
        pairs[s, i].start()

    def combine(s, i, there):
        pairs[s, i].wait_recv()
        cols = quarter(there)
        held[s, :, cols] = (part[s, mine, cols].astype(F32) + pair_rx[s, :, cols].astype(F32)).astype(BF16)

    def rs_start(s, i, src, dst, steps):
        rs[s, i] = remote(src, dst, rs_send.at[s, i], rs_recv.at[s, i], along_chip(steps))
        rs[s, i].start()

    def spread(s):
        order = (across, ahead, behind, chip)
        for i, there in enumerate(order):
            project(s, i, there)
        for i, there in enumerate(order):
            combine(s, i, there)
            if i == 0:
                rs_start(s, 0, held.at[s, :, eighth(across, 0)], relay_rx.at[s, 0], 1)
                rs_start(s, 1, held.at[s, :, eighth(across, 1)], relay_rx.at[s, 1], 3)
        rs_start(s, 2, held.at[s, :, eighth(ahead, 1)], sum_rx.at[s, 0], 1)
        rs_start(s, 3, held.at[s, :, eighth(behind, 0)], sum_rx.at[s, 1], 3)

    def relay(s):
        for i, (there, steps) in enumerate(((ahead, 1), (behind, 3))):
            rs[s, i].wait_recv()
            own = held[s, :, eighth(there, i)].astype(F32)
            relay_tx[s, i] = (own + relay_rx[s, i].astype(F32)).astype(BF16)
            rs_start(s, 4 + i, relay_tx.at[s, i], sum_rx.at[s, 2 + i], steps)

    returns = {}

    def reduce(s):
        for i in (2, 3, 4, 5):
            rs[s, i].wait_recv()
        target = home if s == 0 else red
        for half in (0, 1):
            total = held[s, :, eighth(chip, half)].astype(F32)
            total = total + sum_rx[s, 1 - half].astype(F32) + sum_rx[s, 2 + half].astype(F32)
            target[s, :, pl.ds(half * (QUART // 2), QUART // 2)] = total.astype(BF16)
        if s:
            returns[s] = remote(red.at[s], home.at[s], ret_send.at[s], ret_recv.at[s], along_wide(s))
            returns[s].start()

    loads[2].wait()
    loads[3].wait()
    attend(0)
    stage(2)
    loads[4].wait()
    spread(0)
    packs[2].start()
    bnds[2].start()
    relay(0)
    arrive(3)
    attend(3)
    spread(3)
    reduce(0)
    arrive(1)
    attend(1)
    relay(3)
    spread(1)
    reduce(3)
    arrive(2)
    attend(2)
    relay(1)
    spread(2)
    reduce(1)
    relay(2)
    reduce(2)

    for k in (1, 2, 3):
        returns[k].wait_recv()

    here = quarter(chip)
    gathers = []
    for j in (1, 3, 2):
        there = lax.rem(chip + j, CHIPS)
        gather_tx[j] = home[slot_at(there)]
        copy = remote(gather_tx.at[j], out_ref.at[:, here], gather_send.at[j], gather_recv.at[j], along_chip(j))
        copy.start()
        gathers.append(copy)
    out_ref[:, here] = home[slot_at(chip)]

    for k in (1, 2, 3):
        bnds[k].wait_send()
        packs[k].wait_send()
    for s in range(4):
        for i in range(4):
            pairs[s, i].wait_send()
        for i in range(6):
            rs[s, i].wait_send()
        if s:
            returns[s].wait_send()
    for copy in gathers:
        copy.wait_send()
        copy.wait_recv()


def body(queries, resp_kv, prompt_kv, out_weight, lengths, group_prompt):
    queries = queries.reshape(4, RUN, HEADS * HEAD)
    resp_kv = resp_kv.reshape(2, 4, RUN, HEAD)
    hbm = pl.BlockSpec(memory_space=pl.ANY)
    smem = pl.BlockSpec(memory_space=pltpu.SMEM)
    dma = pltpu.SemaphoreType.DMA
    return pl.pallas_call(
        kernel,
        out_shape=jax.ShapeDtypeStruct((HALF, D_OUT), BF16),
        in_specs=[hbm, hbm, hbm, hbm, smem, smem],
        out_specs=pl.BlockSpec(memory_space=pltpu.VMEM),
        scratch_shapes=[
            pltpu.VMEM((4, RUN, HEADS * HEAD), BF16),
            pltpu.VMEM((2, 4, RUN, HEAD), BF16),
            pltpu.VMEM((PROMPT, HEAD), BF16),
            pltpu.VMEM((PROMPT, 2 * HEAD), BF16),
            pltpu.VMEM((HEADS * HEAD, D_OUT), BF16),
            pltpu.VMEM((4, RUN, PACK), BF16),
            pltpu.VMEM((4, RUN, PACK), BF16),
            pltpu.VMEM((4, 8, 128), jnp.int32),
            pltpu.VMEM((4, 8, 128), jnp.int32),
            pltpu.VMEM((4, RUN, 2 * HEAD), BF16),
            pltpu.VMEM((ROWS, KEYS), F32),
            pltpu.VMEM((ROWS, KEYS), F32),
            pltpu.VMEM((ROWS, KEYS), BF16),
            pltpu.VMEM((ROWS, KEYS), BF16),
            pltpu.VMEM((4, RUN, HEADS * HEAD), BF16),
            pltpu.VMEM((4, RUN, D_OUT), BF16),
            pltpu.VMEM((4, HALF, D_OUT), BF16),
            pltpu.VMEM((4, HALF, D_OUT), BF16),
            pltpu.VMEM((4, 2, HALF, QUART // 2), BF16),
            pltpu.VMEM((4, 2, HALF, QUART // 2), BF16),
            pltpu.VMEM((4, 4, HALF, QUART // 2), BF16),
            pltpu.VMEM((4, HALF, QUART), BF16),
            pltpu.VMEM((4, HALF, QUART), BF16),
            pltpu.VMEM((4, HALF, QUART), BF16),
            dma((5,)),
            dma((4,)), dma((4,)), dma((4,)), dma((4,)),
            dma((4, 4)), dma((4, 4)), dma((4, 6)), dma((4, 6)), dma((4,)), dma((4,)), dma((4,)), dma((4,)),
        ],
        compiler_params=pltpu.CompilerParams(
            collective_id=1, has_side_effects=True, vmem_limit_bytes=60 * 1024 * 1024
        ),
        cost_estimate=pl.CostEstimate(flops=9 * 10**9, bytes_accessed=12 * 2**20, transcendentals=9 * 10**6),
    )(queries, resp_kv, prompt_kv, out_weight, lengths, group_prompt)


def solution(mesh):
    placed = (
        P("wide", "tp"),
        P(None, "wide", "tp"),
        P(None, "wide", "tp"),
        P("tp", None),
        P("wide", None),
        P("wide", None),
    )
    return jax.shard_map(
        body, mesh=mesh, in_specs=placed, out_specs=P(("wide", "tp"), None), check_vma=False
    )
```

```python
import functools
import math

import jax
import jax.numpy as jnp
from jax import lax
from jax.experimental import pallas as pl
from jax.experimental.pallas import tpu as pltpu
from jax.sharding import PartitionSpec as P

MESH = pl.DeviceIdType.MESH
HEAD = 128
RUN = 128
HEADS = 8
PROMPT = 2048
KEYS = PROMPT + RUN
D_OUT = 4096
WIDE = 32
CHIPS = 4
HALF = RUN // 2
QUART = D_OUT // CHIPS
MID = QUART // 2
LAST = 3
CHUNK_HEADS = 4
ROWS = CHUNK_HEADS * RUN
PACK = HEADS * HEAD + 2 * HEAD
EXP_SCALE = math.log2(math.e) / math.sqrt(HEAD)
F32 = jnp.float32
BF16 = jnp.bfloat16


def kernel(
    q_hbm, resp_hbm, prompt_hbm, w_hbm, len_ref, gp_ref,
    out_ref,
    q_buf, resp_buf, keys, vals, w_buf,
    pack_tx, pack_rx, bound_tx, bound_rx, self_vals,
    score0, score1, prob0, prob1, att, part, pair_rx, held, relay_rx, relay_tx, sum_rx, red, home_low, home_high, gather_tx,
    load_sem, pack_send, pack_recv, bound_send, bound_recv,
    pair_send, pair_recv, rs_send, rs_recv, ret_send, ret_recv, gather_send, gather_recv,
):
    wide = lax.axis_index("wide")
    member = lax.axis_index("tp")
    chip = lax.div(member, 2)
    core = lax.rem(member, 2)

    loads = [
        pltpu.make_async_copy(q_hbm, q_buf, load_sem.at[0]),
        pltpu.make_async_copy(resp_hbm, resp_buf, load_sem.at[1]),
        pltpu.make_async_copy(prompt_hbm.at[0], keys, load_sem.at[2]),
        pltpu.make_async_copy(prompt_hbm.at[1], vals.at[:, pl.ds(0, HEAD)], load_sem.at[3]),
        pltpu.make_async_copy(w_hbm, w_buf, load_sem.at[4]),
    ]
    for load in loads[:4]:
        load.start()

    def along_wide(steps):
        return {"wide": lax.rem(wide + steps + WIDE, WIDE)}

    def along_chip(steps):
        return {"tp": lax.rem(member + 2 * steps, 2 * CHIPS)}

    sibling = {"tp": member + 1 - 2 * core}

    barrier = pltpu.get_barrier_semaphore()
    partners = [along_wide(s) for s in (-3, -2, -1, 1, 2, 3)] + [along_chip(s) for s in (1, 2, 3)] + [sibling]
    for partner in partners:
        pl.semaphore_signal(barrier, inc=1, device_id=partner, device_id_type=MESH)

    def remote(src, dst, send, recv, device):
        return pltpu.make_async_remote_copy(
            src_ref=src, dst_ref=dst, send_sem=send, recv_sem=recv, device_id=device, device_id_type=MESH
        )

    def slot_at(block):
        return jnp.minimum(lax.rem(wide - gp_ref[0, block] + WIDE, WIDE), 3)

    slot_of = [slot_at(b) for b in range(4)]
    hit = [[1 - jnp.minimum((slot_of[b] - k) * (slot_of[b] - k), 1) for b in range(4)] for k in range(4)]
    block_of = [jnp.minimum(hit[k][1] + 2 * hit[k][2] + 3 * hit[k][3], 3) for k in range(4)]

    vals[:, pl.ds(HEAD, HEAD)] = jnp.ones((PROMPT, HEAD), BF16)
    for s in range(4):
        self_vals[s, :, pl.ds(HEAD, HEAD)] = jnp.ones((RUN, HEAD), BF16)

    loads[0].wait()
    loads[1].wait()
    loads[4].start()
    line = lax.broadcasted_iota(jnp.int32, (8, 128), 0)

    def stage(k):
        target = pack_rx if k == 0 else pack_tx
        bounds = bound_rx if k == 0 else bound_tx
        target[k, :, pl.ds(0, HEADS * HEAD)] = q_buf[block_of[k]]
        target[k, :, pl.ds(HEADS * HEAD, HEAD)] = resp_buf[0, block_of[k]]
        target[k, :, pl.ds((HEADS + 1) * HEAD, HEAD)] = resp_buf[1, block_of[k]]
        first = sum(hit[k][b] * len_ref[b, 0] for b in range(4))
        second = first + sum(hit[k][b] * len_ref[b, 1] for b in range(4))
        third = second + sum(hit[k][b] * len_ref[b, 2] for b in range(4))
        bounds[k] = jnp.where(line == 0, first, jnp.where(line == 1, second, third))

    bnds = {
        k: remote(bound_tx.at[k], bound_rx.at[k], bound_send.at[k], bound_recv.at[k], along_wide(-k)) for k in (1, 2, 3)
    }
    packs = {
        k: remote(pack_tx.at[k], pack_rx.at[k], pack_send.at[k], pack_recv.at[k], along_wide(-k)) for k in (1, 2, 3)
    }

    stage(1)
    pl.semaphore_wait(barrier, len(partners))

    packs[1].start()
    stage(3)
    packs[3].start()
    bnds[1].start()
    bnds[3].start()
    stage(0)

    column = lax.rem(wide, CHIPS)
    differs = 1 - jnp.minimum((column - 1) * (column - 1), 1)
    turn = (0, 3 - 2 * differs, 1 + differs, 2 + differs)

    def arrive(s):
        k = turn[s]
        back = along_wide(-k)
        remote(bound_tx.at[k], bound_rx.at[k], bound_send.at[k], bound_recv.at[k], back).wait_recv()
        remote(pack_tx.at[k], pack_rx.at[k], pack_send.at[k], pack_recv.at[k], back).wait_recv()

    def make_scores(s, chunk, score):
        rows = jnp.concatenate(
            [pack_rx[turn[s], :, pl.ds((chunk * CHUNK_HEADS + j) * HEAD, HEAD)] for j in range(CHUNK_HEADS)], axis=0
        )
        dims = (((1,), (1,)), ((), ()))
        score[:, pl.ds(0, PROMPT)] = lax.dot_general(rows, keys[...], dims, preferred_element_type=F32)
        score[:, pl.ds(PROMPT, RUN)] = lax.dot_general(
            rows, pack_rx[turn[s], :, pl.ds(HEADS * HEAD, HEAD)], dims, preferred_element_type=F32
        )

    def make_mask(s):
        at = lax.broadcasted_iota(jnp.int32, (RUN, RUN), 0)
        key_at = lax.broadcasted_iota(jnp.int32, (RUN, RUN), 1)
        begin = jnp.zeros((RUN, RUN), jnp.int32)
        for j in range(3):
            edge = bound_rx[turn[s], pl.ds(j, 1), :]
            begin = jnp.maximum(begin, jnp.where(at >= edge, edge, 0))
        return (key_at >= begin) & (key_at <= at)

    def finish(s, chunk, score, prob):
        mask = make_mask(s)
        for j in range(CHUNK_HEADS):
            here = pl.ds(j * RUN, RUN)
            far = score[here, pl.ds(0, PROMPT)]
            near = jnp.where(mask, score[here, pl.ds(PROMPT, RUN)], -jnp.inf)
            top = jnp.maximum(jnp.max(far, axis=1, keepdims=True), jnp.max(near, axis=1, keepdims=True))
            top = top * EXP_SCALE
            prob[here, pl.ds(0, PROMPT)] = jnp.exp2(far * EXP_SCALE - top).astype(BF16)
            prob[here, pl.ds(PROMPT, RUN)] = jnp.exp2(near * EXP_SCALE - top).astype(BF16)
        mixed = jnp.dot(prob[:, pl.ds(0, PROMPT)], vals[...], preferred_element_type=F32)
        mixed = mixed + jnp.dot(prob[:, pl.ds(PROMPT, RUN)], self_vals[s], preferred_element_type=F32)
        result = (mixed[:, :HEAD] / mixed[:, HEAD:]).astype(BF16)
        for j in range(CHUNK_HEADS):
            att[s, :, pl.ds((chunk * CHUNK_HEADS + j) * HEAD, HEAD)] = result[j * RUN:(j + 1) * RUN]

    def attend(s):
        self_vals[s, :, pl.ds(0, HEAD)] = pack_rx[turn[s], :, pl.ds((HEADS + 1) * HEAD, HEAD)]
        make_scores(s, 0, score0)
        make_scores(s, 1, score1)
        finish(s, 0, score0, prob0)
        finish(s, 1, score1, prob1)

    ahead, behind = lax.rem(chip + 1, CHIPS), lax.rem(chip + CHIPS - 1, CHIPS)
    across = lax.rem(chip + 2, CHIPS)
    mine = pl.ds(pl.multiple_of(core * HALF, HALF), HALF)
    theirs = pl.ds(pl.multiple_of((1 - core) * HALF, HALF), HALF)

    def span(there, start, width):
        return pl.ds(pl.multiple_of(there * QUART + start, HEAD), width)

    def piece(s, p):
        return (p * MID, MID) if s == LAST else (0, QUART)

    pairs, rs, returns = {}, {}, {}
    order = (across, ahead, behind, chip)

    def project(s, p):
        start, width = piece(s, p)
        for i, there in enumerate(order):
            cols = span(there, start, width)
            part[s, :, cols] = jnp.dot(att[s], w_buf[:, cols], preferred_element_type=F32).astype(BF16)
            pairs[s, p, i] = remote(
                part.at[s, theirs, cols], pair_rx.at[s, :, cols], pair_send.at[s, p, i], pair_recv.at[s, p, i], sibling
            )
            pairs[s, p, i].start()

    def rs_start(s, p, i, src, dst, steps):
        rs[s, p, i] = remote(src, dst, rs_send.at[s, p, i], rs_recv.at[s, p, i], along_chip(steps))
        rs[s, p, i].start()

    def portion(s, p, there, half):
        start, width = piece(s, p)
        return span(there, start + half * (width // 2), width // 2)

    def slots(s, p):
        width = piece(s, p)[1] // 2
        return pl.ds(p * width, width)

    def combine(s, p, i):
        pairs[s, p, i].wait_recv()
        cols = span(order[i], *piece(s, p))
        held[s, :, cols] = (part[s, mine, cols].astype(F32) + pair_rx[s, :, cols].astype(F32)).astype(BF16)

    def combine_far(s, p):
        combine(s, p, 0)
        there = slots(s, p)
        rs_start(s, p, 0, held.at[s, :, portion(s, p, across, 0)], relay_rx.at[s, 0, :, there], 1)
        rs_start(s, p, 1, held.at[s, :, portion(s, p, across, 1)], relay_rx.at[s, 1, :, there], 3)

    def combine_near(s, p):
        for i in (1, 2, 3):
            combine(s, p, i)
        there = slots(s, p)
        rs_start(s, p, 2, held.at[s, :, portion(s, p, ahead, 1)], sum_rx.at[s, 0, :, there], 1)
        rs_start(s, p, 3, held.at[s, :, portion(s, p, behind, 0)], sum_rx.at[s, 1, :, there], 3)

    def relay(s, p):
        there = slots(s, p)
        for i, (goal, steps) in enumerate(((ahead, 1), (behind, 3))):
            rs[s, p, i].wait_recv()
            own = held[s, :, portion(s, p, goal, i)].astype(F32)
            relay_tx[s, i, :, there] = (own + relay_rx[s, i, :, there].astype(F32)).astype(BF16)
            rs_start(s, p, 4 + i, relay_tx.at[s, i, :, there], sum_rx.at[s, 2 + i, :, there], steps)

    homes = (home_low, home_high)

    def reduce(s, p):
        for i in (2, 3, 4, 5):
            rs[s, p, i].wait_recv()
        there = slots(s, p)
        start, width = piece(s, p)
        for half in (0, 1):
            total = held[s, :, portion(s, p, chip, half)].astype(F32)
            total = total + sum_rx[s, 1 - half, :, there].astype(F32) + sum_rx[s, 2 + half, :, there].astype(F32)
            at = start + half * (width // 2)
            if s == 0:
                homes[half][s] = total.astype(BF16)
            else:
                red[s, :, pl.ds(at, width // 2)] = total.astype(BF16)
        if s:
            for h in ((p,) if s == LAST else (0, 1)):
                k = turn[s]
                returns[s, h] = remote(
                    red.at[s, :, pl.ds(h * MID, MID)], homes[h].at[k], ret_send.at[s, h], ret_recv.at[k, h], along_wide(k)
                )
                returns[s, h].start()

    loads[2].wait()
    loads[3].wait()
    attend(0)
    stage(2)
    loads[4].wait()
    project(0, 0)
    combine_far(0, 0)
    combine_near(0, 0)

    @pl.when(column != 0)
    def _():
        packs[2].start()
        bnds[2].start()

    relay(0, 0)
    arrive(1)
    attend(1)

    @pl.when(column == 0)
    def _():
        packs[2].start()
        bnds[2].start()

    project(1, 0)
    combine_far(1, 0)
    combine_near(1, 0)
    reduce(0, 0)
    arrive(2)
    attend(2)
    relay(1, 0)
    project(2, 0)
    combine_far(2, 0)
    combine_near(2, 0)
    reduce(1, 0)
    arrive(3)
    attend(3)
    relay(2, 0)
    project(3, 0)
    combine_far(3, 0)
    project(3, 1)
    combine_near(3, 0)
    combine_far(3, 1)
    combine_near(3, 1)
    relay(3, 0)
    reduce(2, 0)
    relay(3, 1)
    reduce(3, 0)
    reduce(3, 1)

    gathers = []
    for h in (0, 1):
        for k in (1, 3, 2):
            remote(
                red.at[k, :, pl.ds(h * MID, MID)], homes[h].at[k], ret_send.at[k, h], ret_recv.at[k, h], along_wide(k)
            ).wait_recv()
        here = span(chip, h * MID, MID)
        for j in (1, 3, 2):
            gather_tx[h, j] = homes[h][slot_at(lax.rem(chip + j, CHIPS))]
            copy = remote(
                gather_tx.at[h, j], out_ref.at[:, here], gather_send.at[h, j], gather_recv.at[h, j], along_chip(j)
            )
            copy.start()
            gathers.append(copy)
        out_ref[:, here] = homes[h][slot_at(chip)]

    for k in (1, 2, 3):
        bnds[k].wait_send()
        packs[k].wait_send()
    for copy in list(pairs.values()) + list(rs.values()) + list(returns.values()):
        copy.wait_send()
    for copy in gathers:
        copy.wait_send()
        copy.wait_recv()


def body(queries, resp_kv, prompt_kv, out_weight, lengths, group_prompt):
    queries = queries.reshape(4, RUN, HEADS * HEAD)
    resp_kv = resp_kv.reshape(2, 4, RUN, HEAD)
    hbm = pl.BlockSpec(memory_space=pl.ANY)
    smem = pl.BlockSpec(memory_space=pltpu.SMEM)
    dma = pltpu.SemaphoreType.DMA
    return pl.pallas_call(
        kernel,
        out_shape=jax.ShapeDtypeStruct((HALF, D_OUT), BF16),
        in_specs=[hbm, hbm, hbm, hbm, smem, smem],
        out_specs=pl.BlockSpec(memory_space=pltpu.VMEM),
        scratch_shapes=[
            pltpu.VMEM((4, RUN, HEADS * HEAD), BF16),
            pltpu.VMEM((2, 4, RUN, HEAD), BF16),
            pltpu.VMEM((PROMPT, HEAD), BF16),
            pltpu.VMEM((PROMPT, 2 * HEAD), BF16),
            pltpu.VMEM((HEADS * HEAD, D_OUT), BF16),
            pltpu.VMEM((4, RUN, PACK), BF16),
            pltpu.VMEM((4, RUN, PACK), BF16),
            pltpu.VMEM((4, 8, 128), jnp.int32),
            pltpu.VMEM((4, 8, 128), jnp.int32),
            pltpu.VMEM((4, RUN, 2 * HEAD), BF16),
            pltpu.VMEM((ROWS, KEYS), F32),
            pltpu.VMEM((ROWS, KEYS), F32),
            pltpu.VMEM((ROWS, KEYS), BF16),
            pltpu.VMEM((ROWS, KEYS), BF16),
            pltpu.VMEM((4, RUN, HEADS * HEAD), BF16),
            pltpu.VMEM((4, RUN, D_OUT), BF16),
            pltpu.VMEM((4, HALF, D_OUT), BF16),
            pltpu.VMEM((4, HALF, D_OUT), BF16),
            pltpu.VMEM((4, 2, HALF, QUART // 2), BF16),
            pltpu.VMEM((4, 2, HALF, QUART // 2), BF16),
            pltpu.VMEM((4, 4, HALF, QUART // 2), BF16),
            pltpu.VMEM((4, HALF, QUART), BF16),
            pltpu.VMEM((4, HALF, MID), BF16),
            pltpu.VMEM((4, HALF, MID), BF16),
            pltpu.VMEM((2, 4, HALF, MID), BF16),
            dma((5,)),
            dma((4,)), dma((4,)), dma((4,)), dma((4,)),
            dma((4, 2, 4)), dma((4, 2, 4)), dma((4, 2, 6)), dma((4, 2, 6)),
            dma((4, 2)), dma((4, 2)), dma((2, 4)), dma((2, 4)),
        ],
        compiler_params=pltpu.CompilerParams(
            collective_id=1, has_side_effects=True, vmem_limit_bytes=60 * 1024 * 1024
        ),
        cost_estimate=pl.CostEstimate(flops=9 * 10**9, bytes_accessed=12 * 2**20, transcendentals=9 * 10**6),
    )(queries, resp_kv, prompt_kv, out_weight, lengths, group_prompt)


def solution(mesh):
    placed = (
        P("wide", "tp"),
        P(None, "wide", "tp"),
        P(None, "wide", "tp"),
        P("tp", None),
        P("wide", None),
        P("wide", None),
    )
    return jax.shard_map(
        body, mesh=mesh, in_specs=placed, out_specs=P(("wide", "tp"), None), check_vma=False
    )
```
